32 devices in a mesh: outer: 4 (over y, x), inner: 8 (over z, core).
Axes of the slice: x: 2, y: 2, z: 4, core: 2. Of those that a mesh axis runs over, the one named last changes fastest.
Arguments:
- frames: bfloat16 [16384, 1536], P(('outer', 'inner')), may hold values from -6 to 6
- w_qkv: bfloat16 [1536, 2304], replicated, may hold values from -64 to 64, as said below
- w_out: bfloat16 [768, 1536], replicated, may hold values from -0.21875 to 0.21875
- w_point: bfloat16 [1536, 3072], replicated, may hold values from -0.15625 to 0.15625
- conv_kernel: float32 [31, 1536], replicated, may hold values from -1 to 1
Outputs:
- block_out: bfloat16 [16384, 1536], P(('outer', 'inner'))
The draws below stay inside these ranges and needn't reach their ends.
Inputs may be any that keep to these rules, and one draw needn't show every extreme that they name: `w_qkv`: the query, key and value projections side by side, 768 columns each.
All inputs are finite; a program needn't handle non-finite values.
Results may differ from the reference program's by a relative error of at most 0.005.
The reference program's roundings to bfloat16 on the way count: a program that leaves them out, or rounds other values in their place, can miss the bound.
Values may be sent and summed in bfloat16 or wider, within the bound.
A program may use at most 128 MiB of HBM per device.

```python
import math
import jax
import jax.numpy as jnp
from jax import lax

D = 1536
HEADS = 12
HEAD_DIM = 64
KW = 31
TOK_DEV = 512
HD = 768
WINDOW = 1024
FRAMES = 16384


def draw_frames(key, part):
    key = jax.random.fold_in(key, 5)
    key_common = jax.random.fold_in(key, 0)
    values = jax.random.truncated_normal(key_common, -6.0, 6.0, (FRAMES, D), jnp.float32)
    values = values.at[0, 0].set(6.0).at[1, 0].set(-6.0)
    return values.astype(jnp.bfloat16)


def draw_w_qkv(key, part):
    key = jax.random.fold_in(key, 11)
    key_query, key_other, key_value = jax.random.split(key, 3)
    query_part = jax.random.truncated_normal(key_query, -6.0, 6.0, (D, HEADS * HEAD_DIM), jnp.float32)
    key_noise = jax.random.truncated_normal(key_other, -6.0, 6.0, (D, HEADS * HEAD_DIM), jnp.float32)
    value_part = jax.random.truncated_normal(key_value, -6.0, 6.0, (D, HEADS * HEAD_DIM), jnp.float32) / math.sqrt(D)
    query_part = query_part * math.sqrt(2.0 / D)
    key_part = key_noise * math.sqrt(2.0 / D)
    return jnp.concatenate([query_part, key_part, value_part], 1).astype(jnp.bfloat16)


def normal_values(stream_key, dims, width, most, kind=jnp.bfloat16):
    values = jax.random.normal(stream_key, dims, jnp.float32) * width
    return jnp.minimum(jnp.maximum(values, -most), most).astype(kind)


def setup_inputs(seed: int = 0) -> dict:
    keys = jax.random.split(jax.random.key(seed), 6)
    frames = draw_frames(jax.random.fold_in(keys[5], 71), 0)
    w_qkv = draw_w_qkv(jax.random.fold_in(keys[5], 71), 0)
    w_out = normal_values(keys[2], (HD, D), HD ** -0.5, 0.21875)
    w_point = normal_values(keys[3], (D, 2 * D), D ** -0.5, 0.15625)
    conv_kernel = normal_values(keys[4], (KW, D), KW ** -0.5, 1.0, jnp.float32)
    return dict(frames=frames, w_qkv=w_qkv, w_out=w_out, w_point=w_point, conv_kernel=conv_kernel)


def layer_norm(values):
    average = lax.optimization_barrier(jnp.mean(values, -1, keepdims=True))
    centred = values - average
    return centred * lax.rsqrt(lax.optimization_barrier(jnp.mean(centred * centred, -1, keepdims=True)) + 1e-05)

def attend(queries, keyvals, query_pos, key_pos, total_frames):
    query_count = queries.shape[0]
    key_count = keyvals.shape[0]
    allowed = (jnp.abs(query_pos[:, None] - key_pos[None, :]) <= WINDOW) & (key_pos[None, :] >= 0) & (key_pos[None, :] < total_frames)
    head_queries = queries.reshape(query_count, HEADS, HEAD_DIM).transpose(1, 0, 2)
    head_keys = keyvals[:, :HD].reshape(key_count, HEADS, HEAD_DIM).transpose(1, 0, 2)
    head_values = keyvals[:, HD:].reshape(key_count, HEADS, HEAD_DIM).transpose(1, 0, 2)

    def one_head(operands):
        query_part, key_part, value_part = operands
        scores = jnp.dot(query_part, key_part.T, preferred_element_type=jnp.float32) * HEAD_DIM ** (-0.5)
        scores = jnp.where(allowed, scores, -1e+30)
        highest = lax.optimization_barrier(jnp.max(scores, -1, keepdims=True))
        expo = jnp.exp(scores - highest)
        totals = lax.optimization_barrier(jnp.sum(expo, -1, keepdims=True))
        weighted = jnp.dot(expo.astype(jnp.bfloat16), value_part, preferred_element_type=jnp.float32)
        return (weighted / totals).astype(jnp.bfloat16)
    result = lax.map(one_head, (head_queries, head_keys, head_values))
    return result.transpose(1, 0, 2).reshape(query_count, HD)

def reference(frames, w_qkv, w_out, w_point, conv_kernel):
    inputs = frames.astype(jnp.float32)
    normed = layer_norm(inputs).astype(jnp.bfloat16)
    projections = jnp.dot(normed, w_qkv, preferred_element_type=jnp.float32).astype(jnp.bfloat16)
    queries = projections[:, :HD]
    keyvals = projections[:, HD:]
    padded = jnp.pad(keyvals, ((2 * TOK_DEV, 2 * TOK_DEV), (0, 0)))
    block_count = FRAMES // TOK_DEV

    def per_block(block_index):
        first_row = (block_index * TOK_DEV).astype(jnp.int32)
        block_queries = lax.dynamic_slice_in_dim(queries, first_row, TOK_DEV, 0)
        block_keys = lax.dynamic_slice_in_dim(padded, first_row, 5 * TOK_DEV, 0)
        query_pos = first_row + jnp.arange(TOK_DEV, dtype=jnp.int32)
        key_pos = first_row - 2 * TOK_DEV + jnp.arange(5 * TOK_DEV, dtype=jnp.int32)
        return attend(block_queries, block_keys, query_pos, key_pos, FRAMES)
    attended = lax.map(per_block, jnp.arange(block_count, dtype=jnp.int32)).reshape(FRAMES, HD)
    after_attention = inputs + jnp.dot(attended, w_out, preferred_element_type=jnp.float32)
    normed_again = layer_norm(after_attention).astype(jnp.bfloat16)
    projected = jnp.dot(normed_again, w_point, preferred_element_type=jnp.float32)
    gated = (projected[:, :D] * jax.nn.sigmoid(projected[:, D:])).astype(jnp.bfloat16)
    half_width = (KW - 1) // 2
    gated_wide = jnp.pad(gated, ((half_width, half_width), (0, 0)))
    depthwise = jnp.zeros((FRAMES, D), jnp.float32)
    for tap in range(KW):
        depthwise = depthwise + conv_kernel[tap][None, :] * gated_wide[tap:tap + FRAMES].astype(jnp.float32)
    return (after_attention + jax.nn.silu(layer_norm(depthwise))).astype(jnp.bfloat16)
```

```python
import functools

import jax
import jax.numpy as jnp
from jax import lax
from jax.experimental import pallas as pl
from jax.experimental.pallas import tpu as pltpu
from jax.sharding import PartitionSpec as P

D = 1536
HEADS = 12
HEAD_DIM = 64
KW = 31
HD = 768
AXES = ("outer", "inner")
LANES = 128
PAIRS = HD // LANES
NEG = -1e30


def layer_norm(values):
    average = jnp.mean(values, -1, keepdims=True)
    centred = values - average
    return centred * lax.rsqrt(jnp.mean(centred * centred, -1, keepdims=True) + 1e-05)


def scores_of(queries, keys):
    return lax.dot_general(
        queries, keys, (((1,), (1,)), ((), ())), preferred_element_type=jnp.float32
    )


def head_queries(pair, lane, head):
    picked = jnp.where((lane >= HEAD_DIM) == (head == 1), pair * HEAD_DIM**-0.5, 0.0)
    return picked.astype(jnp.bfloat16)


def softmax_parts(scores, values, highest):
    for part in scores:
        highest = jnp.maximum(highest, jnp.max(part, -1, keepdims=True))
    totals = 0.0
    weighted = 0.0
    for part, value in zip(scores, values):
        expo = jnp.exp(part - highest)
        totals = totals + jnp.sum(expo, -1, keepdims=True)
        weighted = weighted + jnp.dot(
            expo.astype(jnp.bfloat16), value, preferred_element_type=jnp.float32
        )
    return highest, totals, weighted


def near_kernel(rows, q_ref, k0_ref, k1_ref, v0_ref, v1_ref, acc_ref, high_ref, total_ref):
    lane = lax.broadcasted_iota(jnp.int32, (rows, LANES), 1)
    for start in range(0, q_ref.shape[0], rows):
        here = pl.ds(start, rows)
        pair = q_ref[here, :].astype(jnp.float32)
        found = []
        for head in range(2):
            queries = head_queries(pair, lane, head)
            scores = [scores_of(queries, ref[...]) for ref in (k0_ref, k1_ref)]
            found.append(softmax_parts(scores, (v0_ref[...], v1_ref[...]), NEG))
        second = lane >= HEAD_DIM
        high_ref[here, :] = jnp.where(second, found[1][0], found[0][0])
        total_ref[here, :] = jnp.where(second, found[1][1], found[0][1])
        acc_ref[here, :] = jnp.where(second, found[1][2], found[0][2])


def far_kernel(
    rows, lim_ref, q_ref, ka_ref, kb_ref, kc_ref, va_ref, vb_ref, vc_ref,
    acc_ref, high_ref, total_ref, out_ref,
):
    lane = lax.broadcasted_iota(jnp.int32, (rows, LANES), 1)
    count = q_ref.shape[0]
    for start in range(0, count, rows):
        here = pl.ds(start, rows)
        pair = q_ref[here, :].astype(jnp.float32)
        before = pl.ds(start, count - start)
        after = pl.ds(0, start + rows)
        gap_a = lax.broadcasted_iota(jnp.int32, (rows, count - start), 1) - (
            lax.broadcasted_iota(jnp.int32, (rows, count - start), 0)
        )
        gap_c = lax.broadcasted_iota(jnp.int32, (rows, start + rows), 1) - (
            lax.broadcasted_iota(jnp.int32, (rows, start + rows), 0) + start
        )
        in_a = gap_a >= lim_ref[0]
        in_c = gap_c <= lim_ref[2]
        bias_b = jnp.where(lim_ref[1] > 0, 0.0, NEG)
        found = []
        for head in range(2):
            queries = head_queries(pair, lane, head)
            scores = [
                jnp.where(in_a, scores_of(queries, ka_ref[before, :]), NEG),
                scores_of(queries, kb_ref[...]) + bias_b,
                jnp.where(in_c, scores_of(queries, kc_ref[after, :]), NEG),
            ]
            values = (va_ref[before, :], vb_ref[...], vc_ref[after, :])
            old = high_ref[here, :][:, head * HEAD_DIM : head * HEAD_DIM + 1]
            found.append(softmax_parts(scores, values, old))
        second = lane >= HEAD_DIM
        highest = jnp.where(second, found[1][0], found[0][0])
        scale = jnp.exp(high_ref[here, :] - highest)
        totals = jnp.where(second, found[1][1], found[0][1]) + scale * total_ref[here, :]
        weighted = jnp.where(second, found[1][2], found[0][2]) + scale * acc_ref[here, :]
        out_ref[here, :] = (weighted / totals).astype(jnp.bfloat16)


def conv_kernel_body(
    rows, gated_ref, left_ref, right_ref, after_ref, taps_ref, out_ref, wide_ref, sum_ref
):
    count = gated_ref.shape[0]
    halo = left_ref.shape[0]
    step = pl.program_id(0)
    blocks = D // LANES

    @pl.when(step == 0)
    def _():
        for block in range(blocks):
            cols = pl.ds(block * LANES, LANES)
            wide_ref[block, :halo, :] = left_ref[:, cols].astype(jnp.float32)
            wide_ref[block, pl.ds(halo, count), :] = gated_ref[:, cols].astype(jnp.float32)
            wide_ref[block, pl.ds(halo + count, halo), :] = right_ref[:, cols].astype(jnp.float32)

    first = pl.multiple_of(step * rows, rows)
    lead = halo - (KW - 1) // 2
    for block in range(blocks):
        cols = pl.ds(block * LANES, LANES)
        total = jnp.zeros((rows, LANES), jnp.float32)
        for tap in range(KW):
            total = total + taps_ref[pl.ds(tap, 1), cols] * (
                wide_ref[block, pl.ds(first + (lead + tap), rows), :]
            )
        sum_ref[:, cols] = total
    normed = layer_norm(sum_ref[...])
    out_ref[...] = (after_ref[...] + normed / (1.0 + jnp.exp(-normed))).astype(jnp.bfloat16)


def call_near(queries, own, other):
    count = queries.shape[0]
    key = pl.BlockSpec((count, LANES), lambda i: (0, i))
    value = pl.BlockSpec((count, LANES), lambda i: (0, i + PAIRS))
    state = jax.ShapeDtypeStruct((count, HD), jnp.float32)
    return pl.pallas_call(
        functools.partial(near_kernel, count // 2),
        grid=(PAIRS,),
        in_specs=[key, key, key, value, value],
        out_specs=[key] * 3,
        out_shape=[state] * 3,
        compiler_params=pltpu.CompilerParams(vmem_limit_bytes=40 << 20),
        cost_estimate=pl.CostEstimate(
            flops=HEADS * 2 * 2 * count * 2 * count * 256,
            bytes_accessed=12 << 20,
            transcendentals=HEADS * count * 2 * count,
        ),
        name="near_attention",
    )(queries, own, other, own, other)


def call_far(limits, queries, a, b, c, state):
    count = queries.shape[0]
    key = pl.BlockSpec((count, LANES), lambda i: (0, i))
    value = pl.BlockSpec((count, LANES), lambda i: (0, i + PAIRS))
    return pl.pallas_call(
        functools.partial(far_kernel, count // 2),
        grid=(PAIRS,),
        in_specs=[pl.BlockSpec(memory_space=pltpu.SMEM)]
        + [key] * 4 + [value] * 3 + [key] * 3,
        out_specs=key,
        out_shape=jax.ShapeDtypeStruct((count, HD), jnp.bfloat16),
        compiler_params=pltpu.CompilerParams(vmem_limit_bytes=40 << 20),
        cost_estimate=pl.CostEstimate(
            flops=HEADS * 2 * 2 * count * 3 * count * 256,
            bytes_accessed=12 << 20,
            transcendentals=HEADS * count * 3 * count,
        ),
        name="far_attention",
    )(limits, queries, a, b, c, a, b, c, *state)


def call_conv(gated, left, right, after, taps):
    count = gated.shape[0]
    halo = left.shape[0]
    rows = 64
    whole = lambda array: pl.BlockSpec(array.shape, lambda i: (0, 0))
    block = pl.BlockSpec((rows, D), lambda i: (i, 0))
    return pl.pallas_call(
        functools.partial(conv_kernel_body, rows),
        grid=(count // rows,),
        in_specs=[whole(gated), whole(left), whole(right), block, whole(taps)],
        out_specs=block,
        out_shape=jax.ShapeDtypeStruct((count, D), jnp.bfloat16),
        scratch_shapes=[
            pltpu.VMEM((D // LANES, count + 2 * halo, LANES), jnp.float32),
            pltpu.VMEM((rows, D), jnp.float32),
        ],
        compiler_params=pltpu.CompilerParams(vmem_limit_bytes=40 << 20),
        name="conv_tail",
    )(gated, left, right, after, taps)


def on_device(frames, w_qkv, w_out, w_point, conv_kernel):
    index = lax.axis_index(AXES)
    total = lax.axis_size(AXES)

    def shifted(array, by):
        pairs = [(i, i + by) for i in range(total) if 0 <= i + by < total]
        return lax.ppermute(array, AXES, pairs)

    def swapped(array):
        return lax.ppermute(array, AXES, [(i, i ^ 1) for i in range(total)])

    inputs = frames.astype(jnp.float32)
    normed = layer_norm(inputs).astype(jnp.bfloat16)
    keyvals = jnp.dot(normed, w_qkv[:, HD:], preferred_element_type=jnp.float32).astype(
        jnp.bfloat16
    )
    from_before = shifted(keyvals, 2)
    from_after = shifted(keyvals, -2)
    other = swapped(keyvals)
    queries = jnp.dot(normed, w_qkv[:, :HD], preferred_element_type=jnp.float32).astype(
        jnp.bfloat16
    )
    even = index % 2 == 0
    state = call_near(queries, keyvals, other)
    from_before, from_after, state = lax.optimization_barrier((from_before, from_after, state))
    bridge = swapped(jnp.where(even, from_after, from_before))
    big = 1 << 20
    limits = jnp.stack([
        jnp.where(index >= 2, 0, big),
        jnp.where(jnp.where(even, index >= 1, index + 1 < total), 1, 0),
        jnp.where(index + 2 < total, 0, -big),
    ]).astype(jnp.int32)
    attended = call_far(limits, queries, from_before, bridge, from_after, state)
    after_attention = inputs + jnp.dot(attended, w_out, preferred_element_type=jnp.float32)
    normed_again = layer_norm(after_attention).astype(jnp.bfloat16)
    projected = jnp.dot(normed_again, w_point, preferred_element_type=jnp.float32)
    gated = (projected[:, :D] * jax.nn.sigmoid(projected[:, D:])).astype(jnp.bfloat16)
    left = shifted(gated[-16:], 1)
    right = shifted(gated[:16], -1)
    return call_conv(gated, left, right, after_attention, conv_kernel)


def solution(mesh):
    return jax.shard_map(
        on_device,
        mesh=mesh,
        in_specs=(P(AXES, None), P(), P(), P(), P()),
        out_specs=P(AXES, None),
        check_vma=False,
    )
```

```python
import functools

import jax
import jax.numpy as jnp
from jax import lax
from jax.experimental import pallas as pl
from jax.experimental.pallas import tpu as pltpu
from jax.sharding import PartitionSpec as P

D = 1536
HEADS = 12
HEAD_DIM = 64
KW = 31
HD = 768
AXES = ("outer", "inner")
LANES = 128
SPLIT = 512
NEG = -1e30


def layer_norm(values):
    average = jnp.mean(values, -1, keepdims=True)
    centred = values - average
    return centred * lax.rsqrt(jnp.mean(centred * centred, -1, keepdims=True) + 1e-05)


def scores_of(queries, keys):
    return lax.dot_general(
        queries, keys, (((1,), (1,)), ((), ())), preferred_element_type=jnp.float32
    )


def head_queries(pair, lane, head):
    picked = jnp.where((lane >= HEAD_DIM) == (head == 1), pair * HEAD_DIM**-0.5, 0.0)
    return picked.astype(jnp.bfloat16)


def softmax_parts(scores, values, highest):
    for part in scores:
        highest = jnp.maximum(highest, jnp.max(part, -1, keepdims=True))
    totals = 0.0
    weighted = 0.0
    for part, value in zip(scores, values):
        expo = jnp.exp(part - highest)
        totals = totals + jnp.sum(expo, -1, keepdims=True)
        weighted = weighted + jnp.dot(
            expo.astype(jnp.bfloat16), value, preferred_element_type=jnp.float32
        )
    return highest, totals, weighted


def near_kernel(rows, q_ref, k0_ref, k1_ref, v0_ref, v1_ref, acc_ref, high_ref, total_ref):
    lane = lax.broadcasted_iota(jnp.int32, (rows, LANES), 1)
    for start in range(0, q_ref.shape[0], rows):
        here = pl.ds(start, rows)
        pair = q_ref[here, :].astype(jnp.float32)
        found = []
        for head in range(2):
            queries = head_queries(pair, lane, head)
            scores = [scores_of(queries, ref[...]) for ref in (k0_ref, k1_ref)]
            found.append(softmax_parts(scores, (v0_ref[...], v1_ref[...]), NEG))
        second = lane >= HEAD_DIM
        high_ref[here, :] = jnp.where(second, found[1][0], found[0][0])
        total_ref[here, :] = jnp.where(second, found[1][1], found[0][1])
        acc_ref[here, :] = jnp.where(second, found[1][2], found[0][2])


def far_kernel(
    rows, lim_ref, q_ref, ka_ref, kb_ref, kc_ref, va_ref, vb_ref, vc_ref,
    acc_ref, high_ref, total_ref, out_ref,
):
    lane = lax.broadcasted_iota(jnp.int32, (rows, LANES), 1)
    count = q_ref.shape[0]
    for start in range(0, count, rows):
        here = pl.ds(start, rows)
        pair = q_ref[here, :].astype(jnp.float32)
        before = pl.ds(start, count - start)
        after = pl.ds(0, start + rows)
        gap_a = lax.broadcasted_iota(jnp.int32, (rows, count - start), 1) - (
            lax.broadcasted_iota(jnp.int32, (rows, count - start), 0)
        )
        gap_c = lax.broadcasted_iota(jnp.int32, (rows, start + rows), 1) - (
            lax.broadcasted_iota(jnp.int32, (rows, start + rows), 0) + start
        )
        in_a = gap_a >= lim_ref[0]
        in_c = gap_c <= lim_ref[2]
        bias_b = jnp.where(lim_ref[1] > 0, 0.0, NEG)
        found = []
        for head in range(2):
            queries = head_queries(pair, lane, head)
            scores = [
                jnp.where(in_a, scores_of(queries, ka_ref[before, :]), NEG),
                scores_of(queries, kb_ref[...]) + bias_b,
                jnp.where(in_c, scores_of(queries, kc_ref[after, :]), NEG),
            ]
            values = (va_ref[before, :], vb_ref[...], vc_ref[after, :])
            old = high_ref[here, :][:, head * HEAD_DIM : head * HEAD_DIM + 1]
            found.append(softmax_parts(scores, values, old))
        second = lane >= HEAD_DIM
        highest = jnp.where(second, found[1][0], found[0][0])
        scale = jnp.exp(high_ref[here, :] - highest)
        totals = jnp.where(second, found[1][1], found[0][1]) + scale * total_ref[here, :]
        weighted = jnp.where(second, found[1][2], found[0][2]) + scale * acc_ref[here, :]
        out_ref[here, :] = (weighted / totals).astype(jnp.bfloat16)


def conv_kernel_body(
    rows, gated_ref, left_ref, right_ref, after_ref, taps_ref, out_ref, wide_ref, sum_ref
):
    count = gated_ref.shape[0]
    halo = left_ref.shape[0]
    step = pl.program_id(0)
    blocks = D // LANES

    @pl.when(step == 0)
    def _():
        for block in range(blocks):
            cols = pl.ds(block * LANES, LANES)
            wide_ref[block, :halo, :] = left_ref[:, cols].astype(jnp.float32)
            wide_ref[block, pl.ds(halo, count), :] = gated_ref[:, cols].astype(jnp.float32)
            wide_ref[block, pl.ds(halo + count, halo), :] = right_ref[:, cols].astype(jnp.float32)

    first = pl.multiple_of(step * rows, rows)
    lead = halo - (KW - 1) // 2
    for block in range(blocks):
        cols = pl.ds(block * LANES, LANES)
        total = jnp.zeros((rows, LANES), jnp.float32)
        for tap in range(KW):
            total = total + taps_ref[pl.ds(tap, 1), cols] * (
                wide_ref[block, pl.ds(first + (lead + tap), rows), :]
            )
        sum_ref[:, cols] = total
    normed = layer_norm(sum_ref[...])
    out_ref[...] = (after_ref[...] + normed / (1.0 + jnp.exp(-normed))).astype(jnp.bfloat16)


def call_near(queries, own, other):
    count, width = queries.shape
    pairs = width // LANES
    key = pl.BlockSpec((count, LANES), lambda i: (0, i))
    value = pl.BlockSpec((count, LANES), lambda i: (0, i + pairs))
    state = jax.ShapeDtypeStruct((count, width), jnp.float32)
    return pl.pallas_call(
        functools.partial(near_kernel, count // 2),
        grid=(pairs,),
        in_specs=[key, key, key, value, value],
        out_specs=[key] * 3,
        out_shape=[state] * 3,
        compiler_params=pltpu.CompilerParams(vmem_limit_bytes=40 << 20),
        cost_estimate=pl.CostEstimate(
            flops=2 * pairs * 2 * 2 * count * 2 * count * 256,
            bytes_accessed=12 << 20,
            transcendentals=2 * pairs * count * 2 * count,
        ),
        name="near_attention",
    )(queries, own, other, own, other)


def call_far(limits, queries, a, b, c, state):
    count, width = queries.shape
    pairs = width // LANES
    key = pl.BlockSpec((count, LANES), lambda i: (0, i))
    value = pl.BlockSpec((count, LANES), lambda i: (0, i + pairs))
    return pl.pallas_call(
        functools.partial(far_kernel, count // 2),
        grid=(pairs,),
        in_specs=[pl.BlockSpec(memory_space=pltpu.SMEM)]
        + [key] * 4 + [value] * 3 + [key] * 3,
        out_specs=key,
        out_shape=jax.ShapeDtypeStruct((count, width), jnp.bfloat16),
        compiler_params=pltpu.CompilerParams(vmem_limit_bytes=40 << 20),
        cost_estimate=pl.CostEstimate(
            flops=2 * pairs * 2 * 2 * count * 3 * count * 256,
            bytes_accessed=12 << 20,
            transcendentals=2 * pairs * count * 3 * count,
        ),
        name="far_attention",
    )(limits, queries, a, b, c, a, b, c, *state)


def call_conv(gated, left, right, after, taps):
    count = gated.shape[0]
    halo = left.shape[0]
    rows = 64
    whole = lambda array: pl.BlockSpec(array.shape, lambda i: (0, 0))
    block = pl.BlockSpec((rows, D), lambda i: (i, 0))
    return pl.pallas_call(
        functools.partial(conv_kernel_body, rows),
        grid=(count // rows,),
        in_specs=[whole(gated), whole(left), whole(right), block, whole(taps)],
        out_specs=block,
        out_shape=jax.ShapeDtypeStruct((count, D), jnp.bfloat16),
        scratch_shapes=[
            pltpu.VMEM((D // LANES, count + 2 * halo, LANES), jnp.float32),
            pltpu.VMEM((rows, D), jnp.float32),
        ],
        compiler_params=pltpu.CompilerParams(vmem_limit_bytes=40 << 20),
        name="conv_tail",
    )(gated, left, right, after, taps)


def on_device(frames, w_qkv, w_out, w_point, conv_kernel):
    index = lax.axis_index(AXES)
    total = lax.axis_size(AXES)

    def shifted(array, by):
        pairs = [(i, i + by) for i in range(total) if 0 <= i + by < total]
        return lax.ppermute(array, AXES, pairs)

    def swapped(array):
        return lax.ppermute(array, AXES, [(i, i ^ 1) for i in range(total)])

    inputs = frames.astype(jnp.float32)
    normed = layer_norm(inputs).astype(jnp.bfloat16)
    def project(start, stop):
        return jnp.dot(
            normed, w_qkv[:, start:stop], preferred_element_type=jnp.float32
        ).astype(jnp.bfloat16)

    def keyvals_of(start, stop):
        return jnp.concatenate(
            [project(HD + start, HD + stop), project(2 * HD + start, 2 * HD + stop)], 1
        )

    big = 1 << 20
    even = index % 2 == 0
    limits = jnp.stack([
        jnp.where(index >= 2, 0, big),
        jnp.where(jnp.where(even, index >= 1, index + 1 < total), 1, 0),
        jnp.where(index + 2 < total, 0, -big),
    ]).astype(jnp.int32)

    wait = lax.optimization_barrier
    kv_1 = keyvals_of(0, SPLIT)
    before_1, after_1 = shifted(kv_1, 2), shifted(kv_1, -2)
    other_1 = swapped(kv_1)
    kv_2 = keyvals_of(SPLIT, HD)
    other_2 = swapped(kv_2)
    queries = project(0, HD)
    queries_1, queries_2 = queries[:, :SPLIT], queries[:, SPLIT:]
    acc_1, high_1, sum_1 = call_near(queries_1, kv_1, other_1)
    acc_2, high_2, sum_2 = call_near(queries_2, kv_2, other_2)
    kv_up, kv_down = kv_2, kv_2
    kv_down, after_1, sum_1, sum_2 = wait((kv_down, after_1, sum_1, sum_2))
    after_2 = shifted(kv_down, -2)
    kv_up, before_1, sum_1 = wait((kv_up, before_1, sum_1))
    before_2 = shifted(kv_up, 2)
    bridge_1 = swapped(jnp.where(even, after_1, before_1))
    attended_1 = call_far(
        limits, queries_1, before_1, bridge_1, after_1, (acc_1, high_1, sum_1)
    )
    before_2, after_2, attended_1 = wait((before_2, after_2, attended_1))
    bridge_2 = swapped(jnp.where(even, after_2, before_2))
    attended_2 = call_far(
        limits, queries_2, before_2, bridge_2, after_2, (acc_2, high_2, sum_2)
    )
    attended = jnp.concatenate([attended_1, attended_2], 1)
    after_attention = inputs + jnp.dot(attended, w_out, preferred_element_type=jnp.float32)
    normed_again = layer_norm(after_attention).astype(jnp.bfloat16)
    projected = jnp.dot(normed_again, w_point, preferred_element_type=jnp.float32)
    gated = (projected[:, :D] * jax.nn.sigmoid(projected[:, D:])).astype(jnp.bfloat16)
    left = shifted(gated[-16:], 1)
    right = shifted(gated[:16], -1)
    return call_conv(gated, left, right, after_attention, conv_kernel)


def solution(mesh):
    return jax.shard_map(
        on_device,
        mesh=mesh,
        in_specs=(P(AXES, None), P(), P(), P(), P()),
        out_specs=P(AXES, None),
        check_vma=False,
    )
```

```python
import functools

import jax
import jax.numpy as jnp
from jax import lax
from jax.experimental import pallas as pl
from jax.experimental.pallas import tpu as pltpu
from jax.sharding import PartitionSpec as P

D = 1536
HEADS = 12
HEAD_DIM = 64
KW = 31
HD = 768
AXES = ("outer", "inner")
LANES = 128
SPLIT = 512
NEG = -1e30


def layer_norm(values):
    average = jnp.mean(values, -1, keepdims=True)
    centred = values - average
    return centred * lax.rsqrt(jnp.mean(centred * centred, -1, keepdims=True) + 1e-05)


def scores_of(queries, keys):
    return lax.dot_general(
        queries, keys, (((1,), (1,)), ((), ())), preferred_element_type=jnp.float32
    )


def head_queries(pair, lane, head):
    picked = jnp.where((lane >= HEAD_DIM) == (head == 1), pair * HEAD_DIM**-0.5, 0.0)
    return picked.astype(jnp.bfloat16)


def softmax_parts(scores, values, highest):
    for part in scores:
        highest = jnp.maximum(highest, jnp.max(part, -1, keepdims=True))
    totals = 0.0
    weighted = 0.0
    for part, value in zip(scores, values):
        expo = jnp.exp(part - highest)
        totals = totals + jnp.sum(expo, -1, keepdims=True)
        weighted = weighted + jnp.dot(
            expo.astype(jnp.bfloat16), value, preferred_element_type=jnp.float32
        )
    return highest, totals, weighted


def near_kernel(rows, q_ref, k0_ref, k1_ref, v0_ref, v1_ref, acc_ref, high_ref, total_ref):
    lane = lax.broadcasted_iota(jnp.int32, (rows, LANES), 1)
    for start in range(0, q_ref.shape[0], rows):
        here = pl.ds(start, rows)
        pair = q_ref[here, :].astype(jnp.float32)
        found = []
        for head in range(2):
            queries = head_queries(pair, lane, head)
            scores = [scores_of(queries, ref[...]) for ref in (k0_ref, k1_ref)]
            found.append(softmax_parts(scores, (v0_ref[...], v1_ref[...]), NEG))
        second = lane >= HEAD_DIM
        high_ref[here, :] = jnp.where(second, found[1][0], found[0][0])
        total_ref[here, :] = jnp.where(second, found[1][1], found[0][1])
        acc_ref[here, :] = jnp.where(second, found[1][2], found[0][2])


def far_kernel(
    rows, lim_ref, q_ref, ka_ref, kb_ref, kc_ref, va_ref, vb_ref, vc_ref,
    acc_ref, high_ref, total_ref, out_ref,
):
    lane = lax.broadcasted_iota(jnp.int32, (rows, LANES), 1)
    count = q_ref.shape[0]
    for start in range(0, count, rows):
        here = pl.ds(start, rows)
        pair = q_ref[here, :].astype(jnp.float32)
        before = pl.ds(start, count - start)
        after = pl.ds(0, start + rows)
        gap_a = lax.broadcasted_iota(jnp.int32, (rows, count - start), 1) - (
            lax.broadcasted_iota(jnp.int32, (rows, count - start), 0)
        )
        gap_c = lax.broadcasted_iota(jnp.int32, (rows, start + rows), 1) - (
            lax.broadcasted_iota(jnp.int32, (rows, start + rows), 0) + start
        )
        in_a = gap_a >= lim_ref[0]
        in_c = gap_c <= lim_ref[2]
        bias_b = jnp.where(lim_ref[1] > 0, 0.0, NEG)
        found = []
        for head in range(2):
            queries = head_queries(pair, lane, head)
            scores = [
                jnp.where(in_a, scores_of(queries, ka_ref[before, :]), NEG),
                scores_of(queries, kb_ref[...]) + bias_b,
                jnp.where(in_c, scores_of(queries, kc_ref[after, :]), NEG),
            ]
            values = (va_ref[before, :], vb_ref[...], vc_ref[after, :])
            old = high_ref[here, :][:, head * HEAD_DIM : head * HEAD_DIM + 1]
            found.append(softmax_parts(scores, values, old))
        second = lane >= HEAD_DIM
        highest = jnp.where(second, found[1][0], found[0][0])
        scale = jnp.exp(high_ref[here, :] - highest)
        totals = jnp.where(second, found[1][1], found[0][1]) + scale * total_ref[here, :]
        weighted = jnp.where(second, found[1][2], found[0][2]) + scale * acc_ref[here, :]
        out_ref[here, :] = (weighted / totals).astype(jnp.bfloat16)


def conv_kernel_body(
    rows, gated_ref, left_ref, right_ref, after_ref, taps_ref, out_ref, wide_ref, sum_ref
):
    count = gated_ref.shape[0]
    halo = left_ref.shape[0]
    step = pl.program_id(0)
    blocks = D // LANES

    @pl.when(step == 0)
    def _():
        for block in range(blocks):
            cols = pl.ds(block * LANES, LANES)
            wide_ref[block, :halo, :] = left_ref[:, cols].astype(jnp.float32)
            wide_ref[block, pl.ds(halo, count), :] = gated_ref[:, cols].astype(jnp.float32)
            wide_ref[block, pl.ds(halo + count, halo), :] = right_ref[:, cols].astype(jnp.float32)

    first = pl.multiple_of(step * rows, rows)
    lead = halo - (KW - 1) // 2
    for block in range(blocks):
        cols = pl.ds(block * LANES, LANES)
        total = jnp.zeros((rows, LANES), jnp.float32)
        for tap in range(KW):
            total = total + taps_ref[pl.ds(tap, 1), cols] * (
                wide_ref[block, pl.ds(first + (lead + tap), rows), :]
            )
        sum_ref[:, cols] = total
    normed = layer_norm(sum_ref[...])
    out_ref[...] = (after_ref[...] + normed / (1.0 + jnp.exp(-normed))).astype(jnp.bfloat16)


def call_near(queries, own, other):
    count, width = queries.shape
    pairs = width // LANES
    key = pl.BlockSpec((count, LANES), lambda i: (0, i))
    value = pl.BlockSpec((count, LANES), lambda i: (0, i + pairs))
    state = jax.ShapeDtypeStruct((count, width), jnp.float32)
    return pl.pallas_call(
        functools.partial(near_kernel, count // 2),
        grid=(pairs,),
        in_specs=[key, key, key, value, value],
        out_specs=[key] * 3,
        out_shape=[state] * 3,
        compiler_params=pltpu.CompilerParams(vmem_limit_bytes=40 << 20),
        cost_estimate=pl.CostEstimate(
            flops=pairs * count * 2 * count,
            bytes_accessed=1 << 20,
            transcendentals=0,
        ),
        name="near_attention",
    )(queries, own, other, own, other)


def call_far(limits, queries, a, b, c, state):
    count, width = queries.shape
    pairs = width // LANES
    key = pl.BlockSpec((count, LANES), lambda i: (0, i))
    value = pl.BlockSpec((count, LANES), lambda i: (0, i + pairs))
    return pl.pallas_call(
        functools.partial(far_kernel, count // 2),
        grid=(pairs,),
        in_specs=[pl.BlockSpec(memory_space=pltpu.SMEM)]
        + [key] * 4 + [value] * 3 + [key] * 3,
        out_specs=key,
        out_shape=jax.ShapeDtypeStruct((count, width), jnp.bfloat16),
        compiler_params=pltpu.CompilerParams(vmem_limit_bytes=40 << 20),
        cost_estimate=pl.CostEstimate(
            flops=pairs * count * 3 * count,
            bytes_accessed=1 << 20,
            transcendentals=0,
        ),
        name="far_attention",
    )(limits, queries, a, b, c, a, b, c, *state)


def call_conv(gated, left, right, after, taps):
    count = gated.shape[0]
    halo = left.shape[0]
    rows = 64
    whole = lambda array: pl.BlockSpec(array.shape, lambda i: (0, 0))
    block = pl.BlockSpec((rows, D), lambda i: (i, 0))
    return pl.pallas_call(
        functools.partial(conv_kernel_body, rows),
        grid=(count // rows,),
        in_specs=[whole(gated), whole(left), whole(right), block, whole(taps)],
        out_specs=block,
        out_shape=jax.ShapeDtypeStruct((count, D), jnp.bfloat16),
        scratch_shapes=[
            pltpu.VMEM((D // LANES, count + 2 * halo, LANES), jnp.float32),
            pltpu.VMEM((rows, D), jnp.float32),
        ],
        compiler_params=pltpu.CompilerParams(vmem_limit_bytes=40 << 20),
        name="conv_tail",
    )(gated, left, right, after, taps)


def on_device(frames, w_qkv, w_out, w_point, conv_kernel):
    index = lax.axis_index(AXES)
    total = lax.axis_size(AXES)

    def shifted(array, by):
        pairs = [(i, i + by) for i in range(total) if 0 <= i + by < total]
        return lax.ppermute(array, AXES, pairs)

    def swapped(array):
        return lax.ppermute(array, AXES, [(i, i ^ 1) for i in range(total)])

    inputs = frames.astype(jnp.float32)
    normed = layer_norm(inputs).astype(jnp.bfloat16)
    def project(start, stop):
        return jnp.dot(
            normed, w_qkv[:, start:stop], preferred_element_type=jnp.float32
        ).astype(jnp.bfloat16)

    def keyvals_of(start, stop):
        return jnp.concatenate(
            [project(HD + start, HD + stop), project(2 * HD + start, 2 * HD + stop)], 1
        )

    big = 1 << 20
    even = index % 2 == 0
    limits = jnp.stack([
        jnp.where(index >= 2, 0, big),
        jnp.where(jnp.where(even, index >= 1, index + 1 < total), 1, 0),
        jnp.where(index + 2 < total, 0, -big),
    ]).astype(jnp.int32)

    wait = lax.optimization_barrier
    kv_1 = keyvals_of(0, SPLIT)
    before_1, after_1 = shifted(kv_1, 2), shifted(kv_1, -2)
    other_1 = swapped(kv_1)
    kv_2 = keyvals_of(SPLIT, HD)
    other_2 = swapped(kv_2)
    queries = project(0, HD)
    queries_1, queries_2 = queries[:, :SPLIT], queries[:, SPLIT:]
    acc_1, high_1, sum_1 = call_near(queries_1, kv_1, other_1)
    acc_2, high_2, sum_2 = call_near(queries_2, kv_2, other_2)
    kv_up, kv_down = kv_2, kv_2
    kv_down, after_1, sum_1, sum_2 = wait((kv_down, after_1, sum_1, sum_2))
    after_2 = shifted(kv_down, -2)
    kv_up, before_1, sum_1 = wait((kv_up, before_1, sum_1))
    before_2 = shifted(kv_up, 2)
    bridge_1 = swapped(jnp.where(even, after_1, before_1))
    attended_1 = call_far(
        limits, queries_1, before_1, bridge_1, after_1, (acc_1, high_1, sum_1)
    )
    before_2, after_2, attended_1 = wait((before_2, after_2, attended_1))
    bridge_2 = swapped(jnp.where(even, after_2, before_2))
    attended_2 = call_far(
        limits, queries_2, before_2, bridge_2, after_2, (acc_2, high_2, sum_2)
    )
    attended = jnp.concatenate([attended_1, attended_2], 1)
    after_attention = inputs + jnp.dot(attended, w_out, preferred_element_type=jnp.float32)
    normed_again = layer_norm(after_attention).astype(jnp.bfloat16)
    projected = jnp.dot(normed_again, w_point, preferred_element_type=jnp.float32)
    gated = (projected[:, :D] * jax.nn.sigmoid(projected[:, D:])).astype(jnp.bfloat16)
    left = shifted(gated[-16:], 1)
    right = shifted(gated[:16], -1)
    return call_conv(gated, left, right, after_attention, conv_kernel)


def solution(mesh):
    return jax.shard_map(
        on_device,
        mesh=mesh,
        in_specs=(P(AXES, None), P(), P(), P(), P()),
        out_specs=P(AXES, None),
        check_vma=False,
    )
```

```python
import functools

import jax
import jax.numpy as jnp
from jax import lax
from jax.experimental import pallas as pl
from jax.experimental.pallas import tpu as pltpu
from jax.sharding import PartitionSpec as P

D = 1536
HEADS = 12
HEAD_DIM = 64
KW = 31
HD = 768
AXES = ("outer", "inner")
LANES = 128
SPLIT = 512
NEG = -1e30


def layer_norm(values):
    average = jnp.mean(values, -1, keepdims=True)
    centred = values - average
    return centred * lax.rsqrt(jnp.mean(centred * centred, -1, keepdims=True) + 1e-05)


def scores_of(queries, keys):
    return lax.dot_general(
        queries, keys, (((1,), (1,)), ((), ())), preferred_element_type=jnp.float32
    )


def head_queries(pair, lane, head):
    picked = jnp.where((lane >= HEAD_DIM) == (head == 1), pair * HEAD_DIM**-0.5, 0.0)
    return picked.astype(jnp.bfloat16)


def softmax_parts(scores, values, highest):
    for part in scores:
        highest = jnp.maximum(highest, jnp.max(part, -1, keepdims=True))
    totals = 0.0
    weighted = 0.0
    for part, value in zip(scores, values):
        expo = jnp.exp(part - highest)
        totals = totals + jnp.sum(expo, -1, keepdims=True)
        weighted = weighted + jnp.dot(
            expo.astype(jnp.bfloat16), value, preferred_element_type=jnp.float32
        )
    return highest, totals, weighted


def near_kernel(rows, q_ref, k0_ref, k1_ref, v0_ref, v1_ref, acc_ref, high_ref, total_ref):
    lane = lax.broadcasted_iota(jnp.int32, (rows, LANES), 1)
    for start in range(0, q_ref.shape[0], rows):
        here = pl.ds(start, rows)
        pair = q_ref[here, :].astype(jnp.float32)
        found = []
        for head in range(2):
            queries = head_queries(pair, lane, head)
            scores = [scores_of(queries, ref[...]) for ref in (k0_ref, k1_ref)]
            found.append(softmax_parts(scores, (v0_ref[...], v1_ref[...]), NEG))
        second = lane >= HEAD_DIM
        high_ref[here, :] = jnp.where(second, found[1][0], found[0][0])
        total_ref[here, :] = jnp.where(second, found[1][1], found[0][1])
        acc_ref[here, :] = jnp.where(second, found[1][2], found[0][2])


def far_kernel(
    rows, lim_ref, q_ref, ka_ref, kb_ref, kc_ref, va_ref, vb_ref, vc_ref,
    acc_ref, high_ref, total_ref, out_ref,
):
    lane = lax.broadcasted_iota(jnp.int32, (rows, LANES), 1)
    count = q_ref.shape[0]
    for start in range(0, count, rows):
        here = pl.ds(start, rows)
        pair = q_ref[here, :].astype(jnp.float32)
        before = pl.ds(start, count - start)
        after = pl.ds(0, start + rows)
        gap_a = lax.broadcasted_iota(jnp.int32, (rows, count - start), 1) - (
            lax.broadcasted_iota(jnp.int32, (rows, count - start), 0)
        )
        gap_c = lax.broadcasted_iota(jnp.int32, (rows, start + rows), 1) - (
            lax.broadcasted_iota(jnp.int32, (rows, start + rows), 0) + start
        )
        in_a = gap_a >= lim_ref[0]
        in_c = gap_c <= lim_ref[2]
        bias_b = jnp.where(lim_ref[1] > 0, 0.0, NEG)
        found = []
        for head in range(2):
            queries = head_queries(pair, lane, head)
            scores = [
                jnp.where(in_a, scores_of(queries, ka_ref[before, :]), NEG),
                scores_of(queries, kb_ref[...]) + bias_b,
                jnp.where(in_c, scores_of(queries, kc_ref[after, :]), NEG),
            ]
            values = (va_ref[before, :], vb_ref[...], vc_ref[after, :])
            old = high_ref[here, :][:, head * HEAD_DIM : head * HEAD_DIM + 1]
            found.append(softmax_parts(scores, values, old))
        second = lane >= HEAD_DIM
        highest = jnp.where(second, found[1][0], found[0][0])
        scale = jnp.exp(high_ref[here, :] - highest)
        totals = jnp.where(second, found[1][1], found[0][1]) + scale * total_ref[here, :]
        weighted = jnp.where(second, found[1][2], found[0][2]) + scale * acc_ref[here, :]
        out_ref[here, :] = (weighted / totals).astype(jnp.bfloat16)


def conv_kernel_body(
    rows, gated_ref, left_ref, right_ref, after_ref, taps_ref, out_ref, wide_ref, sum_ref
):
    count = gated_ref.shape[0]
    halo = left_ref.shape[0]
    step = pl.program_id(0)
    blocks = D // LANES

    @pl.when(step == 0)
    def _():
        for block in range(blocks):
            cols = pl.ds(block * LANES, LANES)
            wide_ref[block, :halo, :] = left_ref[:, cols].astype(jnp.float32)
            wide_ref[block, pl.ds(halo, count), :] = gated_ref[:, cols].astype(jnp.float32)
            wide_ref[block, pl.ds(halo + count, halo), :] = right_ref[:, cols].astype(jnp.float32)

    first = pl.multiple_of(step * rows, rows)
    lead = halo - (KW - 1) // 2
    for block in range(blocks):
        cols = pl.ds(block * LANES, LANES)
        total = jnp.zeros((rows, LANES), jnp.float32)
        for tap in range(KW):
            total = total + taps_ref[pl.ds(tap, 1), cols] * (
                wide_ref[block, pl.ds(first + (lead + tap), rows), :]
            )
        sum_ref[:, cols] = total
    normed = layer_norm(sum_ref[...])
    out_ref[...] = (after_ref[...] + normed / (1.0 + jnp.exp(-normed))).astype(jnp.bfloat16)


def call_near(queries, own, other):
    count, width = queries.shape
    pairs = width // LANES
    key = pl.BlockSpec((count, LANES), lambda i: (0, i))
    value = pl.BlockSpec((count, LANES), lambda i: (0, i + pairs))
    state = jax.ShapeDtypeStruct((count, width), jnp.float32)
    return pl.pallas_call(
        functools.partial(near_kernel, count // 2),
        grid=(pairs,),
        in_specs=[key, key, key, value, value],
        out_specs=[key] * 3,
        out_shape=[state] * 3,
        compiler_params=pltpu.CompilerParams(vmem_limit_bytes=40 << 20),
        cost_estimate=pl.CostEstimate(
            flops=pairs * count * 2 * count,
            bytes_accessed=1 << 20,
            transcendentals=0,
        ),
        name="near_attention",
    )(queries, own, other, own, other)


def call_far(limits, queries, a, b, c, state):
    count, width = queries.shape
    pairs = width // LANES
    key = pl.BlockSpec((count, LANES), lambda i: (0, i))
    value = pl.BlockSpec((count, LANES), lambda i: (0, i + pairs))
    return pl.pallas_call(
        functools.partial(far_kernel, count // 2),
        grid=(pairs,),
        in_specs=[pl.BlockSpec(memory_space=pltpu.SMEM)]
        + [key] * 4 + [value] * 3 + [key] * 3,
        out_specs=key,
        out_shape=jax.ShapeDtypeStruct((count, width), jnp.bfloat16),
        compiler_params=pltpu.CompilerParams(vmem_limit_bytes=40 << 20),
        cost_estimate=pl.CostEstimate(
            flops=pairs * count * 3 * count,
            bytes_accessed=1 << 20,
            transcendentals=0,
        ),
        name="far_attention",
    )(limits, queries, a, b, c, a, b, c, *state)


def call_conv(gated, left, right, after, taps):
    count = gated.shape[0]
    halo = left.shape[0]
    rows = 64
    whole = lambda array: pl.BlockSpec(array.shape, lambda i: (0, 0))
    block = pl.BlockSpec((rows, D), lambda i: (i, 0))
    return pl.pallas_call(
        functools.partial(conv_kernel_body, rows),
        grid=(count // rows,),
        in_specs=[whole(gated), whole(left), whole(right), block, whole(taps)],
        out_specs=block,
        out_shape=jax.ShapeDtypeStruct((count, D), jnp.bfloat16),
        scratch_shapes=[
            pltpu.VMEM((D // LANES, count + 2 * halo, LANES), jnp.float32),
            pltpu.VMEM((rows, D), jnp.float32),
        ],
        compiler_params=pltpu.CompilerParams(vmem_limit_bytes=40 << 20),
        name="conv_tail",
    )(gated, left, right, after, taps)


def on_device(frames, w_qkv, w_out, w_point, conv_kernel):
    index = lax.axis_index(AXES)
    total = lax.axis_size(AXES)

    def shifted(array, by):
        pairs = [(i, i + by) for i in range(total) if 0 <= i + by < total]
        return lax.ppermute(array, AXES, pairs)

    def swapped(array):
        return lax.ppermute(array, AXES, [(i, i ^ 1) for i in range(total)])

    inputs = frames.astype(jnp.float32)
    normed = layer_norm(inputs).astype(jnp.bfloat16)
    def project(start, stop):
        return jnp.dot(
            normed, w_qkv[:, start:stop], preferred_element_type=jnp.float32
        ).astype(jnp.bfloat16)

    def keyvals_of(start, stop):
        return jnp.concatenate(
            [project(HD + start, HD + stop), project(2 * HD + start, 2 * HD + stop)], 1
        )

    big = 1 << 20
    even = index % 2 == 0
    limits = jnp.stack([
        jnp.where(index >= 2, 0, big),
        jnp.where(jnp.where(even, index >= 1, index + 1 < total), 1, 0),
        jnp.where(index + 2 < total, 0, -big),
    ]).astype(jnp.int32)

    wait = lax.optimization_barrier
    kv_1 = keyvals_of(0, SPLIT)
    before_1, after_1 = shifted(kv_1, 2), shifted(kv_1, -2)
    other_1 = swapped(kv_1)
    kv_2 = keyvals_of(SPLIT, HD)
    other_2 = swapped(kv_2)
    queries = project(0, HD)
    queries_1, queries_2 = queries[:, :SPLIT], queries[:, SPLIT:]
    acc_1, high_1, sum_1 = call_near(queries_1, kv_1, other_1)
    acc_2, high_2, sum_2 = call_near(queries_2, kv_2, other_2)
    kv_far, sum_1, sum_2 = wait((kv_2, sum_1, sum_2))
    before_2, after_2 = shifted(kv_far, 2), shifted(kv_far, -2)
    bridge_1 = swapped(jnp.where(even, after_1, before_1))
    attended_1 = call_far(
        limits, queries_1, before_1, bridge_1, after_1, (acc_1, high_1, sum_1)
    )
    before_2, after_2, attended_1 = wait((before_2, after_2, attended_1))
    bridge_2 = swapped(jnp.where(even, after_2, before_2))
    attended_2 = call_far(
        limits, queries_2, before_2, bridge_2, after_2, (acc_2, high_2, sum_2)
    )
    attended = jnp.concatenate([attended_1, attended_2], 1)
    after_attention = inputs + jnp.dot(attended, w_out, preferred_element_type=jnp.float32)
    normed_again = layer_norm(after_attention).astype(jnp.bfloat16)
    projected = jnp.dot(normed_again, w_point, preferred_element_type=jnp.float32)
    gated = (projected[:, :D] * jax.nn.sigmoid(projected[:, D:])).astype(jnp.bfloat16)
    left = shifted(gated[-16:], 1)
    right = shifted(gated[:16], -1)
    return call_conv(gated, left, right, after_attention, conv_kernel)


def solution(mesh):
    return jax.shard_map(
        on_device,
        mesh=mesh,
        in_specs=(P(AXES, None), P(), P(), P(), P()),
        out_specs=P(AXES, None),
        check_vma=False,
    )
```

```python
import functools

import jax
import jax.numpy as jnp
from jax import lax
from jax.experimental import pallas as pl
from jax.experimental.pallas import tpu as pltpu
from jax.sharding import PartitionSpec as P

D = 1536
HEADS = 12
HEAD_DIM = 64
KW = 31
HD = 768
AXES = ("outer", "inner")
LANES = 128
SPLIT = 512
NEG = -1e30


def layer_norm(values):
    average = jnp.mean(values, -1, keepdims=True)
    centred = values - average
    return centred * lax.rsqrt(jnp.mean(centred * centred, -1, keepdims=True) + 1e-05)


def scores_of(queries, keys):
    return lax.dot_general(
        queries, keys, (((1,), (1,)), ((), ())), preferred_element_type=jnp.float32
    )


def head_queries(pair, lane, head):
    picked = jnp.where((lane >= HEAD_DIM) == (head == 1), pair * HEAD_DIM**-0.5, 0.0)
    return picked.astype(jnp.bfloat16)


def softmax_parts(scores, values, highest):
    for part in scores:
        highest = jnp.maximum(highest, jnp.max(part, -1, keepdims=True))
    totals = 0.0
    weighted = 0.0
    for part, value in zip(scores, values):
        expo = jnp.exp(part - highest)
        totals = totals + jnp.sum(expo, -1, keepdims=True)
        weighted = weighted + jnp.dot(
            expo.astype(jnp.bfloat16), value, preferred_element_type=jnp.float32
        )
    return highest, totals, weighted


def near_kernel(rows, q_ref, k0_ref, k1_ref, v0_ref, v1_ref, acc_ref, high_ref, total_ref):
    lane = lax.broadcasted_iota(jnp.int32, (rows, LANES), 1)
    for start in range(0, q_ref.shape[0], rows):
        here = pl.ds(start, rows)
        pair = q_ref[here, :].astype(jnp.float32)
        found = []
        for head in range(2):
            queries = head_queries(pair, lane, head)
            scores = [scores_of(queries, ref[...]) for ref in (k0_ref, k1_ref)]
            found.append(softmax_parts(scores, (v0_ref[...], v1_ref[...]), NEG))
        second = lane >= HEAD_DIM
        high_ref[here, :] = jnp.where(second, found[1][0], found[0][0])
        total_ref[here, :] = jnp.where(second, found[1][1], found[0][1])
        acc_ref[here, :] = jnp.where(second, found[1][2], found[0][2])


def far_kernel(
    rows, lim_ref, q_ref, ka_ref, kb_ref, kc_ref, va_ref, vb_ref, vc_ref,
    acc_ref, high_ref, total_ref, out_ref,
):
    lane = lax.broadcasted_iota(jnp.int32, (rows, LANES), 1)
    count = q_ref.shape[0]
    for start in range(0, count, rows):
        here = pl.ds(start, rows)
        pair = q_ref[here, :].astype(jnp.float32)
        before = pl.ds(start, count - start)
        after = pl.ds(0, start + rows)
        gap_a = lax.broadcasted_iota(jnp.int32, (rows, count - start), 1) - (
            lax.broadcasted_iota(jnp.int32, (rows, count - start), 0)
        )
        gap_c = lax.broadcasted_iota(jnp.int32, (rows, start + rows), 1) - (
            lax.broadcasted_iota(jnp.int32, (rows, start + rows), 0) + start
        )
        in_a = gap_a >= lim_ref[0]
        in_c = gap_c <= lim_ref[2]
        bias_b = jnp.where(lim_ref[1] > 0, 0.0, NEG)
        found = []
        for head in range(2):
            queries = head_queries(pair, lane, head)
            scores = [
                jnp.where(in_a, scores_of(queries, ka_ref[before, :]), NEG),
                scores_of(queries, kb_ref[...]) + bias_b,
                jnp.where(in_c, scores_of(queries, kc_ref[after, :]), NEG),
            ]
            values = (va_ref[before, :], vb_ref[...], vc_ref[after, :])
            old = high_ref[here, :][:, head * HEAD_DIM : head * HEAD_DIM + 1]
            found.append(softmax_parts(scores, values, old))
        second = lane >= HEAD_DIM
        highest = jnp.where(second, found[1][0], found[0][0])
        scale = jnp.exp(high_ref[here, :] - highest)
        totals = jnp.where(second, found[1][1], found[0][1]) + scale * total_ref[here, :]
        weighted = jnp.where(second, found[1][2], found[0][2]) + scale * acc_ref[here, :]
        out_ref[here, :] = (weighted / totals).astype(jnp.bfloat16)


def conv_kernel_body(
    rows, halo, inner, total, gated_ref, after_ref, taps_ref, out_ref,
    wide_ref, sum_ref, edge_ref, got_ref, send_sem, recv_sem,
):
    count = gated_ref.shape[0]
    step = pl.program_id(0)
    steps = count // rows
    blocks = D // LANES
    me = lax.axis_index("outer") * inner + lax.axis_index("inner")
    has_before, has_after = me > 0, me < total - 1
    before, after = lax.rem(me + total - 1, total), lax.rem(me + 1, total)
    before = (lax.div(before, inner), lax.rem(before, inner))
    after = (lax.div(after, inner), lax.rem(after, inner))
    sides = ((has_before, before), (has_after, after))
    barrier = pltpu.get_barrier_semaphore()

    def sending(side, device):
        return pltpu.make_async_remote_copy(
            src_ref=edge_ref.at[side],
            dst_ref=got_ref.at[1 - side],
            send_sem=send_sem.at[side],
            recv_sem=recv_sem.at[1 - side],
            device_id=device,
            device_id_type=pl.DeviceIdType.MESH,
        )

    @pl.when(step == 0)
    def _():
        for present, device in sides:
            @pl.when(present)
            def _():
                pl.semaphore_signal(
                    barrier, inc=1, device_id=device, device_id_type=pl.DeviceIdType.MESH
                )

        edge_ref[0, :, :] = gated_ref[pl.ds(0, halo), :]
        edge_ref[1, :, :] = gated_ref[pl.ds(count - halo, halo), :]
        for block in range(blocks):
            cols = pl.ds(block * LANES, LANES)
            wide_ref[block, pl.ds(halo, count), :] = gated_ref[:, cols].astype(jnp.float32)
        pl.semaphore_wait(barrier, has_before.astype(jnp.int32) + has_after.astype(jnp.int32))
        for side, (present, device) in enumerate(sides):
            @pl.when(present)
            def _():
                sending(side, device).start()

    @pl.when(step == steps - 2)
    def _():
        for side, (present, device) in enumerate(sides):
            place = pl.ds(side * (halo + count), halo)

            @pl.when(present)
            def _():
                sending(side, device).wait_send()
                sending(1 - side, device).wait_recv()
                for block in range(blocks):
                    cols = pl.ds(block * LANES, LANES)
                    wide_ref[block, place, :] = got_ref[side, :, cols].astype(jnp.float32)

            @pl.when(jnp.logical_not(present))
            def _():
                for block in range(blocks):
                    wide_ref[block, place, :] = jnp.zeros((halo, LANES), jnp.float32)

    first = pl.multiple_of(lax.rem(step + 1, steps) * rows, rows)
    lead = halo - (KW - 1) // 2
    for block in range(blocks):
        cols = pl.ds(block * LANES, LANES)
        total_sum = jnp.zeros((rows, LANES), jnp.float32)
        for tap in range(KW):
            total_sum = total_sum + taps_ref[pl.ds(tap, 1), cols] * (
                wide_ref[block, pl.ds(first + (lead + tap), rows), :]
            )
        sum_ref[:, cols] = total_sum
    normed = layer_norm(sum_ref[...])
    out_ref[...] = (after_ref[...] + normed / (1.0 + jnp.exp(-normed))).astype(jnp.bfloat16)


def call_near(queries, own, other):
    count, width = queries.shape
    pairs = width // LANES
    key = pl.BlockSpec((count, LANES), lambda i: (0, i))
    value = pl.BlockSpec((count, LANES), lambda i: (0, i + pairs))
    state = jax.ShapeDtypeStruct((count, width), jnp.float32)
    return pl.pallas_call(
        functools.partial(near_kernel, count // 2),
        grid=(pairs,),
        in_specs=[key, key, key, value, value],
        out_specs=[key] * 3,
        out_shape=[state] * 3,
        compiler_params=pltpu.CompilerParams(vmem_limit_bytes=40 << 20),
        cost_estimate=pl.CostEstimate(
            flops=pairs * count * 2 * count,
            bytes_accessed=1 << 20,
            transcendentals=0,
        ),
        name="near_attention",
    )(queries, own, other, own, other)


def call_far(limits, queries, a, b, c, state):
    count, width = queries.shape
    pairs = width // LANES
    key = pl.BlockSpec((count, LANES), lambda i: (0, i))
    value = pl.BlockSpec((count, LANES), lambda i: (0, i + pairs))
    return pl.pallas_call(
        functools.partial(far_kernel, count // 2),
        grid=(pairs,),
        in_specs=[pl.BlockSpec(memory_space=pltpu.SMEM)]
        + [key] * 4 + [value] * 3 + [key] * 3,
        out_specs=key,
        out_shape=jax.ShapeDtypeStruct((count, width), jnp.bfloat16),
        compiler_params=pltpu.CompilerParams(vmem_limit_bytes=40 << 20),
        cost_estimate=pl.CostEstimate(
            flops=pairs * count * 3 * count,
            bytes_accessed=1 << 20,
            transcendentals=0,
        ),
        name="far_attention",
    )(limits, queries, a, b, c, a, b, c, *state)


def call_conv(gated, after, taps):
    count = gated.shape[0]
    halo = 16
    rows = 64
    steps = count // rows
    inner = lax.axis_size("inner")
    whole = lambda array: pl.BlockSpec(array.shape, lambda i: (0, 0))
    block = pl.BlockSpec((rows, D), lambda i: (lax.rem(i + 1, steps), 0))
    return pl.pallas_call(
        functools.partial(conv_kernel_body, rows, halo, inner, inner * lax.axis_size("outer")),
        grid=(steps,),
        in_specs=[whole(gated), block, whole(taps)],
        out_specs=block,
        out_shape=jax.ShapeDtypeStruct((count, D), jnp.bfloat16),
        scratch_shapes=[
            pltpu.VMEM((D // LANES, count + 2 * halo, LANES), jnp.float32),
            pltpu.VMEM((rows, D), jnp.float32),
            pltpu.VMEM((2, halo, D), jnp.bfloat16),
            pltpu.VMEM((2, halo, D), jnp.bfloat16),
            pltpu.SemaphoreType.DMA((2,)),
            pltpu.SemaphoreType.DMA((2,)),
        ],
        compiler_params=pltpu.CompilerParams(
            vmem_limit_bytes=40 << 20, collective_id=0, has_side_effects=True
        ),
        name="conv_tail",
    )(gated, after, taps)


def on_device(frames, w_qkv, w_out, w_point, conv_kernel):
    index = lax.axis_index(AXES)
    total = lax.axis_size(AXES)

    def shifted(array, by):
        pairs = [(i, i + by) for i in range(total) if 0 <= i + by < total]
        return lax.ppermute(array, AXES, pairs)

    def swapped(array):
        return lax.ppermute(array, AXES, [(i, i ^ 1) for i in range(total)])

    inputs = frames.astype(jnp.float32)
    normed = layer_norm(inputs).astype(jnp.bfloat16)
    def project(start, stop):
        return jnp.dot(
            normed, w_qkv[:, start:stop], preferred_element_type=jnp.float32
        ).astype(jnp.bfloat16)

    def keyvals_of(start, stop):
        return jnp.concatenate(
            [project(HD + start, HD + stop), project(2 * HD + start, 2 * HD + stop)], 1
        )

    big = 1 << 20
    even = index % 2 == 0
    limits = jnp.stack([
        jnp.where(index >= 2, 0, big),
        jnp.where(jnp.where(even, index >= 1, index + 1 < total), 1, 0),
        jnp.where(index + 2 < total, 0, -big),
    ]).astype(jnp.int32)

    wait = lax.optimization_barrier
    kv_1 = keyvals_of(0, SPLIT)
    before_1, after_1 = shifted(kv_1, 2), shifted(kv_1, -2)
    other_1 = swapped(kv_1)
    kv_2 = keyvals_of(SPLIT, HD)
    other_2 = swapped(kv_2)
    queries = project(0, HD)
    queries_1, queries_2 = queries[:, :SPLIT], queries[:, SPLIT:]
    acc_1, high_1, sum_1 = call_near(queries_1, kv_1, other_1)
    acc_2, high_2, sum_2 = call_near(queries_2, kv_2, other_2)
    kv_up, kv_down = kv_2, kv_2
    kv_down, after_1, sum_1, sum_2 = wait((kv_down, after_1, sum_1, sum_2))
    after_2 = shifted(kv_down, -2)
    kv_up, before_1, sum_1 = wait((kv_up, before_1, sum_1))
    before_2 = shifted(kv_up, 2)
    bridge_1 = swapped(jnp.where(even, after_1, before_1))
    attended_1 = call_far(
        limits, queries_1, before_1, bridge_1, after_1, (acc_1, high_1, sum_1)
    )
    before_2, after_2, attended_1 = wait((before_2, after_2, attended_1))
    bridge_2 = swapped(jnp.where(even, after_2, before_2))
    attended_2 = call_far(
        limits, queries_2, before_2, bridge_2, after_2, (acc_2, high_2, sum_2)
    )
    attended = jnp.concatenate([attended_1, attended_2], 1)
    after_attention = inputs + jnp.dot(attended, w_out, preferred_element_type=jnp.float32)
    normed_again = layer_norm(after_attention).astype(jnp.bfloat16)
    projected = jnp.dot(normed_again, w_point, preferred_element_type=jnp.float32)
    gated = (projected[:, :D] * jax.nn.sigmoid(projected[:, D:])).astype(jnp.bfloat16)
    return call_conv(gated, after_attention, conv_kernel)


def solution(mesh):
    return jax.shard_map(
        on_device,
        mesh=mesh,
        in_specs=(P(AXES, None), P(), P(), P(), P()),
        out_specs=P(AXES, None),
        check_vma=False,
    )
```

```python
import functools

import jax
import jax.numpy as jnp
from jax import lax
from jax.experimental import pallas as pl
from jax.experimental.pallas import tpu as pltpu
from jax.sharding import PartitionSpec as P

D = 1536
HEADS = 12
HEAD_DIM = 64
KW = 31
HD = 768
AXES = ("outer", "inner")
LANES = 128
SPLIT = 512
NEG = -1e30


def layer_norm(values):
    average = jnp.mean(values, -1, keepdims=True)
    centred = values - average
    return centred * lax.rsqrt(jnp.mean(centred * centred, -1, keepdims=True) + 1e-05)


def scores_of(queries, keys):
    return lax.dot_general(
        queries, keys, (((1,), (1,)), ((), ())), preferred_element_type=jnp.float32
    )


def head_queries(pair, lane, head):
    picked = jnp.where((lane >= HEAD_DIM) == (head == 1), pair * HEAD_DIM**-0.5, 0.0)
    return picked.astype(jnp.bfloat16)


def softmax_parts(scores, values, highest):
    for part in scores:
        highest = jnp.maximum(highest, jnp.max(part, -1, keepdims=True))
    totals = 0.0
    weighted = 0.0
    for part, value in zip(scores, values):
        expo = jnp.exp(part - highest)
        totals = totals + jnp.sum(expo, -1, keepdims=True)
        weighted = weighted + jnp.dot(
            expo.astype(jnp.bfloat16), value, preferred_element_type=jnp.float32
        )
    return highest, totals, weighted


def near_kernel(rows, q_ref, k0_ref, k1_ref, v0_ref, v1_ref, acc_ref, high_ref, total_ref):
    lane = lax.broadcasted_iota(jnp.int32, (rows, LANES), 1)
    for start in range(0, q_ref.shape[0], rows):
        here = pl.ds(start, rows)
        pair = q_ref[here, :].astype(jnp.float32)
        found = []
        for head in range(2):
            queries = head_queries(pair, lane, head)
            scores = [scores_of(queries, ref[...]) for ref in (k0_ref, k1_ref)]
            found.append(softmax_parts(scores, (v0_ref[...], v1_ref[...]), NEG))
        second = lane >= HEAD_DIM
        high_ref[here, :] = jnp.where(second, found[1][0], found[0][0])
        total_ref[here, :] = jnp.where(second, found[1][1], found[0][1])
        acc_ref[here, :] = jnp.where(second, found[1][2], found[0][2])


def far_kernel(
    rows, lim_ref, q_ref, ka_ref, kb_ref, kc_ref, va_ref, vb_ref, vc_ref,
    acc_ref, high_ref, total_ref, out_ref,
):
    lane = lax.broadcasted_iota(jnp.int32, (rows, LANES), 1)
    count = q_ref.shape[0]
    for start in range(0, count, rows):
        here = pl.ds(start, rows)
        pair = q_ref[here, :].astype(jnp.float32)
        before = pl.ds(start, count - start)
        after = pl.ds(0, start + rows)
        gap_a = lax.broadcasted_iota(jnp.int32, (rows, count - start), 1) - (
            lax.broadcasted_iota(jnp.int32, (rows, count - start), 0)
        )
        gap_c = lax.broadcasted_iota(jnp.int32, (rows, start + rows), 1) - (
            lax.broadcasted_iota(jnp.int32, (rows, start + rows), 0) + start
        )
        in_a = gap_a >= lim_ref[0]
        in_c = gap_c <= lim_ref[2]
        bias_b = jnp.where(lim_ref[1] > 0, 0.0, NEG)
        found = []
        for head in range(2):
            queries = head_queries(pair, lane, head)
            scores = [
                jnp.where(in_a, scores_of(queries, ka_ref[before, :]), NEG),
                scores_of(queries, kb_ref[...]) + bias_b,
                jnp.where(in_c, scores_of(queries, kc_ref[after, :]), NEG),
            ]
            values = (va_ref[before, :], vb_ref[...], vc_ref[after, :])
            old = high_ref[here, :][:, head * HEAD_DIM : head * HEAD_DIM + 1]
            found.append(softmax_parts(scores, values, old))
        second = lane >= HEAD_DIM
        highest = jnp.where(second, found[1][0], found[0][0])
        scale = jnp.exp(high_ref[here, :] - highest)
        totals = jnp.where(second, found[1][1], found[0][1]) + scale * total_ref[here, :]
        weighted = jnp.where(second, found[1][2], found[0][2]) + scale * acc_ref[here, :]
        out_ref[here, :] = (weighted / totals).astype(jnp.bfloat16)


def conv_kernel_body(
    rows, halo, inner, total, gated_ref, after_ref, taps_ref, out_ref,
    wide_ref, sum_ref, edge_ref, got_ref, send_sem, recv_sem,
):
    count = gated_ref.shape[0]
    step = pl.program_id(0)
    steps = count // rows
    blocks = D // LANES
    me = lax.axis_index("outer") * inner + lax.axis_index("inner")
    has_before, has_after = me > 0, me < total - 1
    before, after = lax.rem(me + total - 1, total), lax.rem(me + 1, total)
    before = (lax.div(before, inner), lax.rem(before, inner))
    after = (lax.div(after, inner), lax.rem(after, inner))
    sides = ((has_before, before), (has_after, after))
    barrier = pltpu.get_barrier_semaphore()

    def sending(side, device):
        return pltpu.make_async_remote_copy(
            src_ref=edge_ref.at[side],
            dst_ref=got_ref.at[1 - side],
            send_sem=send_sem.at[side],
            recv_sem=recv_sem.at[1 - side],
            device_id=device,
            device_id_type=pl.DeviceIdType.MESH,
        )

    @pl.when(step == 0)
    def _():
        for present, device in sides:
            @pl.when(present)
            def _():
                pl.semaphore_signal(
                    barrier, inc=1, device_id=device, device_id_type=pl.DeviceIdType.MESH
                )

        edge_ref[0, :, :] = gated_ref[pl.ds(0, halo), :]
        edge_ref[1, :, :] = gated_ref[pl.ds(count - halo, halo), :]
        for block in range(blocks):
            cols = pl.ds(block * LANES, LANES)
            wide_ref[block, pl.ds(halo, count), :] = gated_ref[:, cols].astype(jnp.float32)
        pl.semaphore_wait(barrier, has_before.astype(jnp.int32) + has_after.astype(jnp.int32))
        for side, (present, device) in enumerate(sides):
            @pl.when(present)
            def _():
                sending(side, device).start()

    @pl.when(step == steps - 2)
    def _():
        for side, (present, device) in enumerate(sides):
            place = pl.ds(side * (halo + count), halo)

            @pl.when(present)
            def _():
                sending(side, device).wait_send()
                sending(1 - side, device).wait_recv()
                for block in range(blocks):
                    cols = pl.ds(block * LANES, LANES)
                    wide_ref[block, place, :] = got_ref[side, :, cols].astype(jnp.float32)

            @pl.when(jnp.logical_not(present))
            def _():
                for block in range(blocks):
                    wide_ref[block, place, :] = jnp.zeros((halo, LANES), jnp.float32)

    first = pl.multiple_of(lax.rem(step + 1, steps) * rows, rows)
    lead = halo - (KW - 1) // 2
    for block in range(blocks):
        cols = pl.ds(block * LANES, LANES)
        total_sum = jnp.zeros((rows, LANES), jnp.float32)
        for tap in range(KW):
            total_sum = total_sum + taps_ref[pl.ds(tap, 1), cols] * (
                wide_ref[block, pl.ds(first + (lead + tap), rows), :]
            )
        sum_ref[:, cols] = total_sum
    normed = layer_norm(sum_ref[...])
    out_ref[...] = (after_ref[...] + normed / (1.0 + jnp.exp(-normed))).astype(jnp.bfloat16)


def call_near(queries, own, other):
    count, width = queries.shape
    pairs = width // LANES
    key = pl.BlockSpec((count, LANES), lambda i: (0, i))
    value = pl.BlockSpec((count, LANES), lambda i: (0, i + pairs))
    state = jax.ShapeDtypeStruct((count, width), jnp.float32)
    return pl.pallas_call(
        functools.partial(near_kernel, count // 2),
        grid=(pairs,),
        in_specs=[key, key, key, value, value],
        out_specs=[key] * 3,
        out_shape=[state] * 3,
        compiler_params=pltpu.CompilerParams(vmem_limit_bytes=40 << 20),
        cost_estimate=pl.CostEstimate(
            flops=pairs * count * 2 * count,
            bytes_accessed=1 << 20,
            transcendentals=0,
        ),
        name="near_attention",
    )(queries, own, other, own, other)


def call_far(limits, queries, a, b, c, state):
    count, width = queries.shape
    pairs = width // LANES
    key = pl.BlockSpec((count, LANES), lambda i: (0, i))
    value = pl.BlockSpec((count, LANES), lambda i: (0, i + pairs))
    return pl.pallas_call(
        functools.partial(far_kernel, count // 2),
        grid=(pairs,),
        in_specs=[pl.BlockSpec(memory_space=pltpu.SMEM)]
        + [key] * 4 + [value] * 3 + [key] * 3,
        out_specs=key,
        out_shape=jax.ShapeDtypeStruct((count, width), jnp.bfloat16),
        compiler_params=pltpu.CompilerParams(vmem_limit_bytes=40 << 20),
        cost_estimate=pl.CostEstimate(
            flops=pairs * count * 3 * count,
            bytes_accessed=1 << 20,
            transcendentals=0,
        ),
        name="far_attention",
    )(limits, queries, a, b, c, a, b, c, *state)


def call_conv(gated, after, taps):
    count = gated.shape[0]
    halo = 16
    rows = 128
    steps = count // rows
    inner = lax.axis_size("inner")
    whole = lambda array: pl.BlockSpec(array.shape, lambda i: (0, 0))
    block = pl.BlockSpec((rows, D), lambda i: (lax.rem(i + 1, steps), 0))
    return pl.pallas_call(
        functools.partial(conv_kernel_body, rows, halo, inner, inner * lax.axis_size("outer")),
        grid=(steps,),
        in_specs=[whole(gated), block, whole(taps)],
        out_specs=block,
        out_shape=jax.ShapeDtypeStruct((count, D), jnp.bfloat16),
        scratch_shapes=[
            pltpu.VMEM((D // LANES, count + 2 * halo, LANES), jnp.float32),
            pltpu.VMEM((rows, D), jnp.float32),
            pltpu.VMEM((2, halo, D), jnp.bfloat16),
            pltpu.VMEM((2, halo, D), jnp.bfloat16),
            pltpu.SemaphoreType.DMA((2,)),
            pltpu.SemaphoreType.DMA((2,)),
        ],
        compiler_params=pltpu.CompilerParams(
            vmem_limit_bytes=40 << 20, collective_id=0, has_side_effects=True
        ),
        name="conv_tail",
    )(gated, after, taps)


def on_device(frames, w_qkv, w_out, w_point, conv_kernel):
    index = lax.axis_index(AXES)
    total = lax.axis_size(AXES)

    def shifted(array, by):
        pairs = [(i, i + by) for i in range(total) if 0 <= i + by < total]
        return lax.ppermute(array, AXES, pairs)

    def swapped(array):
        return lax.ppermute(array, AXES, [(i, i ^ 1) for i in range(total)])

    inputs = frames.astype(jnp.float32)
    normed = layer_norm(inputs).astype(jnp.bfloat16)
    def project(start, stop):
        return jnp.dot(
            normed, w_qkv[:, start:stop], preferred_element_type=jnp.float32
        ).astype(jnp.bfloat16)

    def keyvals_of(start, stop):
        return jnp.concatenate(
            [project(HD + start, HD + stop), project(2 * HD + start, 2 * HD + stop)], 1
        )

    big = 1 << 20
    even = index % 2 == 0
    limits = jnp.stack([
        jnp.where(index >= 2, 0, big),
        jnp.where(jnp.where(even, index >= 1, index + 1 < total), 1, 0),
        jnp.where(index + 2 < total, 0, -big),
    ]).astype(jnp.int32)

    wait = lax.optimization_barrier
    kv_1 = keyvals_of(0, SPLIT)
    before_1, after_1 = shifted(kv_1, 2), shifted(kv_1, -2)
    other_1 = swapped(kv_1)
    kv_2 = keyvals_of(SPLIT, HD)
    other_2 = swapped(kv_2)
    queries = project(0, HD)
    queries_1, queries_2 = queries[:, :SPLIT], queries[:, SPLIT:]
    acc_1, high_1, sum_1 = call_near(queries_1, kv_1, other_1)
    acc_2, high_2, sum_2 = call_near(queries_2, kv_2, other_2)
    kv_up, kv_down = kv_2, kv_2
    kv_down, after_1, sum_1, sum_2 = wait((kv_down, after_1, sum_1, sum_2))
    after_2 = shifted(kv_down, -2)
    kv_up, before_1, sum_1 = wait((kv_up, before_1, sum_1))
    before_2 = shifted(kv_up, 2)
    bridge_1 = swapped(jnp.where(even, after_1, before_1))
    attended_1 = call_far(
        limits, queries_1, before_1, bridge_1, after_1, (acc_1, high_1, sum_1)
    )
    before_2, after_2, attended_1 = wait((before_2, after_2, attended_1))
    bridge_2 = swapped(jnp.where(even, after_2, before_2))
    attended_2 = call_far(
        limits, queries_2, before_2, bridge_2, after_2, (acc_2, high_2, sum_2)
    )
    attended = jnp.concatenate([attended_1, attended_2], 1)
    after_attention = inputs + jnp.dot(attended, w_out, preferred_element_type=jnp.float32)
    normed_again = layer_norm(after_attention).astype(jnp.bfloat16)
    projected = jnp.dot(normed_again, w_point, preferred_element_type=jnp.float32)
    gated = (projected[:, :D] * jax.nn.sigmoid(projected[:, D:])).astype(jnp.bfloat16)
    return call_conv(gated, after_attention, conv_kernel)


def solution(mesh):
    return jax.shard_map(
        on_device,
        mesh=mesh,
        in_specs=(P(AXES, None), P(), P(), P(), P()),
        out_specs=P(AXES, None),
        check_vma=False,
    )
```
